1024 devices in a mesh: table: 64 (over y, x, core), sample: 16 (over z).
Axes of the slice: x: 4, y: 8, z: 16, core: 2. Of those that a mesh axis runs over, the one named last changes fastest.
Arguments:
- hist_ids: int32 [16384, 64, 48], P(('table', 'sample')), may hold values from 0 to 2047
- hist_lens: int32 [16384, 64], P(('table', 'sample')), may hold values from 1 to 48, 2048 in all within a row
- table_rows: bfloat16 [131072, 256], P('table'), may hold values from -6 to 6
- imp_user: int32 [262144], P(('table', 'sample')), may hold values from 0 to 255
- item_rows: bfloat16 [262144, 256], P(('table', 'sample')), may hold values from -6 to 6
- labels: int32 [262144], P(('table', 'sample')), may hold values 0 or 1
- w_hidden: bfloat16 [512, 512], replicated, may hold values from -0.25 to 0.25
- b_hidden: float32 [512], replicated, may hold values from -3 to 3
- w_back: bfloat16 [512, 512], replicated, may hold values from -0.25 to 0.25
- w_cross: bfloat16 [512, 512], replicated, may hold values from -0.25 to 0.25
- b_cross: float32 [512], replicated, may hold values from -4 to 4
- norm_gain: float32 [512], replicated, may hold values from 0.25 to 1.75
- w_score: float32 [512], replicated, may hold values from -0.25 to 0.25
Outputs:
- pooled_user: bfloat16 [16384, 256], P(('table', 'sample'))
- scores: float32 [262144], P(('table', 'sample'))
- user_grad: float32 [16384, 256], P(('table', 'sample'))
- item_grad: float32 [262144, 256], P(('table', 'sample'))
The draws below stay inside these ranges and needn't reach their ends.
Inputs may be any that keep to these rules, and one draw needn't show every extreme that they name: `hist_lens`: each user's live ids over all shards number exactly 2048; some user has 48 live ids in one shard. `imp_user`: an impression names one of the 256 users held by the devices of its own table index.
All inputs are finite; a program needn't handle non-finite values. No bound on the sum of `labels` on one device may be relied on, other than what follows from the above.
Results may differ from the reference program's by a relative error of at most 0.02.
Values may be sent and summed in bfloat16 or wider, within the bound.
No kernel may reach another device: no remote copies, remote signals or barrier semaphores. Data moves between devices by JAX's collectives and lax.ppermute only.
A program may use at most 32 MiB of HBM per device.

```python
import math
import jax
import jax.numpy as jnp
import numpy as np
from jax import lax

E = 256
FF = 512
CAP = 48
U_DEV = 16
IMP_DEV = 256
ROWS_DEV = 2048
HIST = 2048
USERS = 16384
IMPS = 262144
ROWS = 131072
N_TABLE = 64
N_SAMPLE = 16
DEVICES = 1024


def touch_ends(result, own_key, low, high):
    spot = [jax.random.randint(jax.random.fold_in(own_key, axis), (), 0, length) for axis, length in enumerate(result.shape)]
    main_axis = result.shape.index(max(result.shape))
    beside = spot[:main_axis] + [(spot[main_axis] + 1) % result.shape[main_axis]] + spot[main_axis + 1:]
    return result.at[tuple(spot)].set(low).at[tuple(beside)].set(high)


def level_of(key, dims, cuts, least, largest):
    def one(dim, blocks):
        steps = jax.random.uniform(jax.random.fold_in(jax.random.fold_in(key, 6), dim), (blocks,), jnp.float32, least / len(cuts), largest / len(cuts))
        return jnp.repeat(jnp.exp(steps), dims[dim] // blocks).reshape((-1,) + (1,) * (len(dims) - dim - 1))

    factor_of = one(*cuts[0])
    for cut in cuts[1:]:
        factor_of = factor_of * one(*cut)
    return factor_of


def rank_bounds(number_of, skew):
    portions = [(1 << 20) // math.isqrt(grade ** skew) + 1 for grade in range(1, number_of + 1)]
    width = 1 + sum(portions) // (1 << 30)
    return np.cumsum(np.array([max(1, weight // width) for weight in portions]))


def skewed_ids(own_key, extent, number_of, lean):
    table = rank_bounds(number_of, lean)
    ticket = jax.random.randint(jax.random.fold_in(own_key, 1), extent, 0, int(table[number_of - 1]))
    rank = jnp.searchsorted(jnp.asarray(table, jnp.int32), ticket, side="right")
    return jax.random.permutation(jax.random.fold_in(own_key, 2), number_of)[rank].astype(jnp.int32)


def split_up(count, total, limit, lean):
    weights = [(1 << 20) // math.isqrt(standing ** lean) + 1 for standing in range(2, count + 1)]
    rest, holding = total - limit - (count - 1), [1] * (count - 1)
    while rest > 0:
        movable = [i for i in range(count - 1) if holding[i] < limit]
        pool, budget = sum([weights[i] for i in movable]), rest
        for i in movable:
            extra = min(limit - holding[i], max(1, budget * weights[i] // pool), rest)
            holding[i] = holding[i] + extra
            rest = rest - extra
    return np.array([limit] + holding)


def ragged_sizes(own_key, amount, total, limit, skew):
    if amount == 2:
        one = jax.random.randint(own_key, (), max(1, total - limit), min(limit, total - 1) + 1)
        return jnp.stack([one, total - one])
    lengths = jnp.asarray(split_up(amount, total, limit, skew), jnp.int32)
    twos = (amount - 1) // 2
    donor, sink = lengths[1:1 + 2 * twos:2], lengths[2:2 + 2 * twos:2]
    room = jnp.minimum(donor - 1, limit - sink)
    moved = jax.random.randint(jax.random.fold_in(own_key, 1), (twos,), 0, 1 << 20) % (room + 1)
    lengths = lengths.at[1:1 + 2 * twos:2].set(donor - moved).at[2:2 + 2 * twos:2].set(sink + moved)
    return lengths[jax.random.permutation(jax.random.fold_in(own_key, 2), amount)]


def noise(stream_key, shape, spread, limit, split=(), held_as=jnp.bfloat16):
    entries = spread * jax.random.normal(stream_key, shape, jnp.float32)
    if split:
        entries = entries * level_of(stream_key, shape, split, -0.22, 0.18)
    return jnp.clip(entries, -limit, limit).astype(held_as)


def setup_inputs(seed: int = 0) -> dict:
    splits = jax.random.split(jax.random.key(seed), 14)
    hist_ids = touch_ends(jax.random.randint(splits[0], (USERS, N_TABLE, CAP), 0, ROWS_DEV), jax.random.fold_in(splits[0], 1), 0, ROWS_DEV - 1).astype(jnp.int32)
    hist_lens = jax.vmap(lambda own: ragged_sizes(own, N_TABLE, HIST, CAP, 2))(jax.random.split(splits[1], USERS)).reshape((USERS, N_TABLE)).astype(jnp.int32)
    table_rows = noise(splits[2], (ROWS, E), 1.0, 6.0, ((0, 64),))
    imp_user = touch_ends(skewed_ids(splits[3], (IMPS,), U_DEV * N_SAMPLE, 2), jax.random.fold_in(splits[3], 3), 0, (U_DEV * N_SAMPLE) - 1).astype(jnp.int32)
    item_rows = noise(splits[4], (IMPS, E), 1.0, 6.0, ((0, 1024),))
    labels = touch_ends((jax.random.randint(splits[5], (IMPS,), 0, 4) < 1).astype(jnp.int32), jax.random.fold_in(splits[5], 1), 0, 1)
    w_hidden = noise(splits[6], (2 * E, FF), (2 * E) ** -0.5, 0.25)
    b_hidden = noise(splits[7], (FF,), 0.5, 3.0, (), jnp.float32)
    w_back = noise(splits[8], (FF, 2 * E), FF ** -0.5, 0.25)
    w_cross = noise(splits[9], (2 * E, 2 * E), (2 * E) ** -0.5, 0.25)
    b_cross = noise(splits[10], (2 * E,), 1.0, 4.0, (), jnp.float32)
    norm_gain = jnp.clip(1.0 + 0.15 * jax.random.normal(splits[11], (2 * E,), jnp.float32), 0.25, 1.75)
    w_score = noise(splits[12], (2 * E,), (2 * E) ** -0.5, 0.25, (), jnp.float32)
    return dict(hist_ids=hist_ids, hist_lens=hist_lens, table_rows=table_rows, imp_user=imp_user, item_rows=item_rows, labels=labels, w_hidden=w_hidden, b_hidden=b_hidden, w_back=w_back, w_cross=w_cross, b_cross=b_cross, norm_gain=norm_gain, w_score=w_score)


def forward(user_in, item_in, w_hidden, b_hidden, w_back, w_cross, b_cross, norm_gain, w_score):
    joined = jnp.concatenate([user_in, item_in], axis=1).astype(jnp.bfloat16)
    hidden = jax.nn.gelu(jnp.dot(joined, w_hidden, preferred_element_type=jnp.float32) + b_hidden).astype(jnp.bfloat16)
    mlp_out = jnp.dot(hidden, w_back, preferred_element_type=jnp.float32)
    lifted = joined.astype(jnp.float32)
    crossed = lifted * (jnp.dot(joined, w_cross, preferred_element_type=jnp.float32) + b_cross)
    summed = lifted + mlp_out + crossed
    row_mean = lax.optimization_barrier(jnp.mean(summed, axis=1, keepdims=True))
    centred = summed - row_mean
    row_var = lax.optimization_barrier(jnp.mean(centred * centred, axis=1, keepdims=True))
    normed = centred * lax.rsqrt(row_var + 1e-05) * norm_gain
    return jnp.dot(normed, w_score, precision=lax.Precision.HIGHEST)

def reference(hist_ids, hist_lens, table_rows, imp_user, item_rows, labels, w_hidden, b_hidden, w_back, w_cross, b_cross, norm_gain, w_score):
    owner_base = jnp.arange(N_TABLE, dtype=jnp.int32) * ROWS_DEV

    def pool_block(pair):
        block_ids, block_lens = pair
        gathered = jnp.take(table_rows, block_ids + owner_base[None, :, None], axis=0)
        live_slots = lax.broadcasted_iota(jnp.int32, block_ids.shape, 2) < block_lens[:, :, None]
        return lax.optimization_barrier(jnp.sum(jnp.where(live_slots[..., None], gathered.astype(jnp.float32), jnp.float32(0.0)), axis=(1, 2)))
    pooled_sum = lax.map(pool_block, (hist_ids.reshape(DEVICES, U_DEV, N_TABLE, CAP), hist_lens.reshape(DEVICES, U_DEV, N_TABLE)))
    pooled_sum = pooled_sum.reshape(USERS, E)
    pooled_user = (pooled_sum * float(HIST) ** (-0.5)).astype(jnp.bfloat16)
    group_rows = IMP_DEV * N_SAMPLE
    offsets = jnp.arange(IMPS, dtype=jnp.int32) // group_rows * (U_DEV * N_SAMPLE)
    global_user = (imp_user + offsets).astype(jnp.int32)
    user_feat = jnp.take(pooled_user, global_user, axis=0)

    def group_step(pair):
        user_block, item_block, label_block = pair

        def score_of(user_in, item_in):
            return forward(user_in, item_in, w_hidden, b_hidden, w_back, w_cross, b_cross, norm_gain, w_score)
        block_scores, pullback = jax.vjp(score_of, user_block.astype(jnp.float32), item_block.astype(jnp.float32))
        score_grad = jax.nn.sigmoid(block_scores) - label_block.astype(jnp.float32)
        user_part, item_part = pullback(score_grad)
        return (block_scores, user_part, item_part)
    groups_count = IMPS // group_rows
    scores, user_part, item_grad = lax.map(group_step, (user_feat.reshape(groups_count, group_rows, E), item_rows.reshape(groups_count, group_rows, E), labels.reshape(groups_count, group_rows)))
    scores = scores.reshape(IMPS)
    user_part = user_part.reshape(IMPS, E)
    item_grad = item_grad.reshape(IMPS, E)
    user_grad = jax.ops.segment_sum(user_part, global_user, num_segments=USERS)
    return (pooled_user, scores, user_grad, item_grad)
```

```python
import jax
import jax.numpy as jnp
from jax import lax
from jax.experimental import pallas as pl
from jax.experimental.pallas import tpu as pltpu
from jax.sharding import PartitionSpec as P

F32 = jnp.float32
BF16 = jnp.bfloat16
LOW = 256
VMEM_LIMIT = 48 * 1024 * 1024


def rows_by_rows(a, b):
    return lax.dot_general(a, b, (((1,), (1,)), ((), ())), preferred_element_type=F32)


def pack_kernel(ids_ref, lens_ref, out_ref):
    users, slots, shards = ids_ref.shape
    ids = ids_ref[...]
    live = lax.broadcasted_iota(jnp.int32, ids.shape, 1) < lens_ref[...][:, None, :]
    ids = jnp.where(live, ids, -1)
    half = users // 2
    words = (ids[:half] & 0xFFFF) | (ids[half:] << 16)
    out_ref[...] = words.reshape(half * slots, shards).T.reshape(out_ref.shape)


def pool_kernel(users, words_ref, table_ref, out_ref, counts_ref):
    sources = words_ref.shape[0]
    positions = 2 * words_ref.shape[2]
    highs = counts_ref.shape[0]
    slots = positions // users
    user_of = lax.broadcasted_iota(jnp.int32, (1, positions), 1) // slots
    high_rows = lax.broadcasted_iota(jnp.int32, (highs * users, positions), 0).astype(F32).astype(BF16)
    low_rows = lax.broadcasted_iota(jnp.int32, (LOW, positions), 0).astype(F32).astype(BF16)
    one, zero = jnp.ones((), BF16), jnp.zeros((), BF16)

    def count(source, carry):
        words = words_ref[source]
        ids = jnp.concatenate([words & 0xFFFF, (words >> 16) & 0xFFFF], axis=1)
        high = ((ids // LOW) * users + user_of).astype(F32).astype(BF16)
        low = (ids % LOW).astype(F32).astype(BF16)
        high_hot = jnp.where(high == high_rows, one, zero)
        low_hot = jnp.where(low == low_rows, one, zero)
        counts = rows_by_rows(high_hot, low_hot).astype(BF16)
        rows = pl.ds(pl.multiple_of(source * users, users), users)
        for part in range(highs):
            counts_ref[part, rows, :] = counts[part * users : (part + 1) * users]
        return carry

    lax.fori_loop(0, sources, count, 0, unroll=2)

    chunk = 16
    for first in range(0, sources, chunk):
        total = None
        for part in range(highs):
            term = jnp.dot(
                counts_ref[part, first * users : (first + chunk) * users, :],
                table_ref[part * LOW : (part + 1) * LOW, :],
                preferred_element_type=F32,
            )
            total = term if total is None else total + term
        out_ref[first : first + chunk] = total.astype(BF16).reshape(chunk, users, total.shape[1])


def dense_kernel(
    rows_ref,
    imp_ref,
    item_ref,
    labels_ref,
    w_hidden_ref,
    b_hidden_ref,
    w_back_ref,
    w_cross_ref,
    b_cross_ref,
    gain_ref,
    w_score_ref,
    scores_ref,
    item_grad_ref,
    per_user_ref,
):
    group_users, width = rows_ref.shape
    imps = item_ref.shape[0]
    picks_t = jnp.where(
        lax.broadcasted_iota(jnp.int32, (group_users, imps), 0) == imp_ref[...], 1.0, 0.0
    ).astype(F32)
    picks = picks_t.T.astype(BF16)
    picks_t = picks_t.astype(BF16)
    user_feat = jnp.dot(picks, rows_ref[...], preferred_element_type=F32).astype(BF16)
    joined = jnp.concatenate([user_feat, item_ref[...]], axis=1)
    lifted = joined.astype(F32)
    pre = jnp.dot(joined, w_hidden_ref[...], preferred_element_type=F32) + b_hidden_ref[...]
    cross = jnp.dot(joined, w_cross_ref[...], preferred_element_type=F32) + b_cross_ref[...]
    k, c = 0.7978845608028654, 0.044715
    square = pre * pre
    tanh = jnp.tanh(k * pre * (1.0 + c * square))
    cdf = 0.5 * (1.0 + tanh)
    hidden = (pre * cdf).astype(BF16)
    slope = cdf + 0.5 * pre * (1.0 - tanh * tanh) * (k * (1.0 + 3.0 * c * square))
    summed = lifted + jnp.dot(hidden, w_back_ref[...], preferred_element_type=F32) + lifted * cross
    columns = summed.shape[1]
    centred = summed - jnp.sum(summed, axis=1, keepdims=True) * (1.0 / columns)
    variance = jnp.sum(centred * centred, axis=1, keepdims=True) * (1.0 / columns)
    scale = lax.rsqrt(variance + 1e-05)
    weight = gain_ref[...] * w_score_ref[...]
    scores = scale * jnp.sum(centred * weight, axis=1, keepdims=True)
    scores_ref[...] = jnp.broadcast_to(scores, (imps, 128)).T[:1]
    labels = jnp.broadcast_to(labels_ref[...].astype(F32), (8, imps)).T[:, :1]
    score_grad = 1.0 / (1.0 + jnp.exp(-scores)) - labels
    flat = weight - jnp.sum(weight, axis=1, keepdims=True) * (1.0 / columns)
    summed_grad = (score_grad * scale) * (flat - centred * (scale * scores * (1.0 / columns)))
    hidden_grad = rows_by_rows(summed_grad.astype(BF16), w_back_ref[...])
    pre_grad = (hidden_grad * slope).astype(BF16)
    cross_grad = (summed_grad * lifted).astype(BF16)
    joined_grad = (
        summed_grad * (1.0 + cross)
        + rows_by_rows(pre_grad, w_hidden_ref[...])
        + rows_by_rows(cross_grad, w_cross_ref[...])
    )
    item_grad_ref[...] = joined_grad[:, width:]
    user_part = joined_grad[:, :width].astype(BF16)
    per_user_ref[...] = jnp.dot(picks_t, user_part, preferred_element_type=F32).astype(BF16)


def kernel_call(kernel, out_shape, flops, scratch=()):
    return pl.pallas_call(
        kernel,
        out_shape=out_shape,
        scratch_shapes=list(scratch),
        compiler_params=pltpu.CompilerParams(vmem_limit_bytes=VMEM_LIMIT),
        cost_estimate=pl.CostEstimate(flops=flops, bytes_accessed=1 << 21, transcendentals=0),
    )


def body(
    hist_ids,
    hist_lens,
    table_rows,
    imp_user,
    item_rows,
    labels,
    w_hidden,
    b_hidden,
    w_back,
    w_cross,
    b_cross,
    norm_gain,
    w_score,
):
    users, sources, slots = hist_ids.shape
    table_count, width = table_rows.shape
    samples = lax.axis_size("sample")
    imps = imp_user.shape[0]
    history = slots * sources * 2 // 3
    with jax.named_scope("pack_ids"):
        words = kernel_call(
            pack_kernel,
            jax.ShapeDtypeStruct((sources, 1, users * slots // 2), jnp.int32),
            1 << 20,
        )(jnp.transpose(hist_ids, (0, 2, 1)), hist_lens)
    words = lax.all_to_all(words, "table", split_axis=0, concat_axis=0, tiled=True)
    with jax.named_scope("pool"):
        partials = kernel_call(
            lambda *refs: pool_kernel(users, *refs),
            jax.ShapeDtypeStruct((sources, users, width), BF16),
            1 << 32,
            [pltpu.VMEM((table_count // LOW, sources * users, LOW), BF16)],
        )(words, table_rows)
    returned = lax.all_to_all(partials, "table", split_axis=0, concat_axis=0, tiled=True)
    pooled_user = (jnp.sum(returned.astype(F32), axis=0) * float(history) ** (-0.5)).astype(BF16)
    group_rows = lax.all_to_all(
        jnp.broadcast_to(pooled_user[None], (samples, users, width)),
        "sample",
        split_axis=0,
        concat_axis=0,
        tiled=True,
    ).reshape(samples * users, width)
    row = lambda vector: vector.reshape(1, -1)
    with jax.named_scope("dense"):
        scores, item_grad, per_user = kernel_call(
            dense_kernel,
            (
                jax.ShapeDtypeStruct((1, imps), F32),
                jax.ShapeDtypeStruct((imps, width), F32),
                jax.ShapeDtypeStruct((samples * users, width), BF16),
            ),
            1 << 30,
        )(
            group_rows,
            row(imp_user),
            item_rows,
            row(labels),
            w_hidden,
            row(b_hidden),
            w_back,
            w_cross,
            row(b_cross),
            row(norm_gain),
            row(w_score),
        )
    parts = lax.all_to_all(
        per_user.reshape(samples, users, width), "sample", split_axis=0, concat_axis=0, tiled=True
    )
    user_grad = jnp.sum(parts.astype(F32), axis=0)
    return (pooled_user, scores.reshape(-1), user_grad, item_grad)


def solution(mesh):
    both = ("table", "sample")
    in_specs = (
        P(both, None, None),
        P(both, None),
        P("table", None),
        P(both),
        P(both, None),
        P(both),
    ) + (P(),) * 7
    out_specs = (P(both, None), P(both), P(both, None), P(both, None))
    return jax.shard_map(body, mesh=mesh, in_specs=in_specs, out_specs=out_specs, check_vma=False)
```

```python
import jax
import jax.numpy as jnp
from jax import lax
from jax.experimental import pallas as pl
from jax.experimental.pallas import tpu as pltpu
from jax.sharding import PartitionSpec as P

F32 = jnp.float32
BF16 = jnp.bfloat16
F8 = jnp.float8_e4m3fn
LOW = 256
VMEM_LIMIT = 48 * 1024 * 1024


def rows_by_rows(a, b):
    return lax.dot_general(a, b, (((1,), (1,)), ((), ())), preferred_element_type=F32)


def pack_words(ids, lens):
    live = lax.broadcasted_iota(jnp.int32, ids.shape, 1) < lens[:, None, :]
    ids = jnp.where(live, ids, -1)
    half = ids.shape[0] // 2
    return (ids[:half] & 0xFFFF) | (ids[half:] << 16)


def turn_kernel(words_ref, out_ref):
    half, slots, shards = words_ref.shape
    words = words_ref[...].reshape(half * slots, shards).T
    chips, cores, _ = out_ref.shape
    for chip in range(chips):
        out_ref[chip] = words[chip * cores : (chip + 1) * cores]


def pool_kernel(users, n_staged, words_ref, other_ref, table_hbm, *refs):
    staged_hbm, (out_ref, *staged_refs) = refs[:n_staged], refs[n_staged : 2 * n_staged + 1]
    counts_ref, table_ref, sems = refs[2 * n_staged + 1 :]
    copies = [pltpu.make_async_copy(table_hbm, table_ref, sems.at[0])]
    for i, (source, target) in enumerate(zip(staged_hbm, staged_refs)):
        copies.append(pltpu.make_async_copy(source, target, sems.at[i + 1]))
    for copy in copies:
        copy.start()
    sources = words_ref.shape[0]
    first_core = lax.rem(lax.axis_index("table"), 2) == 0
    positions = 2 * words_ref.shape[2]
    highs = table_ref.shape[0] // LOW
    slots = positions // users
    user_of = lax.broadcasted_iota(jnp.int32, (1, positions), 1) // slots
    high_rows = lax.broadcasted_iota(jnp.int32, (highs * users, positions), 0).astype(jnp.int8)
    low_rows = (lax.broadcasted_iota(jnp.int32, (LOW, positions), 0) - LOW // 2).astype(jnp.int8)
    one, zero = jnp.ones((), F8), jnp.zeros((), F8)

    def count(source, carry):
        pair = words_ref[source]
        own = jnp.where(first_core, pair[:1], pair[1:])
        other = jnp.where(first_core, pair[1:], pair[:1])
        rows = pl.ds(pl.multiple_of(source * users, users), users)
        for shard, words in enumerate((own, other)):
            ids = jnp.concatenate([words & 0xFFFF, (words >> 16) & 0xFFFF], axis=1)
            high = (ids // LOW) * users + user_of
            high = jnp.where(high < highs * users, high, -1).astype(jnp.int8)
            low = (ids % LOW - LOW // 2).astype(jnp.int8)
            high_hot = jnp.where(high == high_rows, one, zero)
            low_hot = jnp.where(low == low_rows, one, zero)
            counts = rows_by_rows(high_hot, low_hot).astype(BF16)
            for part in range(highs):
                counts_ref[shard * highs + part, rows, :] = counts[part * users : (part + 1) * users]
        return carry

    lax.fori_loop(0, sources, count, 0, unroll=8)
    for copy in copies:
        copy.wait()
    chunk = 16
    for first in range(0, sources, chunk):
        total = None
        for part in range(2 * highs):
            shard_ref = (table_ref, other_ref)[part // highs]
            low_row = part % highs * LOW
            term = jnp.dot(
                counts_ref[part, first * users : (first + chunk) * users, :],
                shard_ref[low_row : low_row + LOW, :],
                preferred_element_type=F32,
            )
            total = term if total is None else total + term
        out_ref[first : first + chunk] = total.astype(BF16).reshape(chunk, users, total.shape[1])


def dense_kernel(
    rows_ref,
    imp_ref,
    item_ref,
    labels_ref,
    w_hidden_ref,
    b_hidden_ref,
    w_back_ref,
    w_cross_ref,
    b_cross_ref,
    gain_ref,
    w_score_ref,
    scores_ref,
    item_grad_ref,
    per_user_ref,
):
    group_users, width = rows_ref.shape
    imps = item_ref.shape[0]
    picks_t = jnp.where(
        lax.broadcasted_iota(jnp.int32, (group_users, imps), 0) == imp_ref[...], 1.0, 0.0
    ).astype(F32)
    picks = picks_t.T.astype(BF16)
    picks_t = picks_t.astype(BF16)
    user_feat = jnp.dot(picks, rows_ref[...], preferred_element_type=F32).astype(BF16)
    joined = jnp.concatenate([user_feat, item_ref[...]], axis=1)
    lifted = joined.astype(F32)
    pre = jnp.dot(joined, w_hidden_ref[...], preferred_element_type=F32) + b_hidden_ref[...]
    cross = jnp.dot(joined, w_cross_ref[...], preferred_element_type=F32) + b_cross_ref[...]
    k, c = 0.7978845608028654, 0.044715
    square = pre * pre
    tanh = jnp.tanh(k * pre * (1.0 + c * square))
    cdf = 0.5 * (1.0 + tanh)
    hidden = (pre * cdf).astype(BF16)
    slope = cdf + 0.5 * pre * (1.0 - tanh * tanh) * (k * (1.0 + 3.0 * c * square))
    summed = lifted + jnp.dot(hidden, w_back_ref[...], preferred_element_type=F32) + lifted * cross
    columns = summed.shape[1]
    centred = summed - jnp.sum(summed, axis=1, keepdims=True) * (1.0 / columns)
    variance = jnp.sum(centred * centred, axis=1, keepdims=True) * (1.0 / columns)
    scale = lax.rsqrt(variance + 1e-05)
    weight = gain_ref[...] * w_score_ref[...]
    scores = scale * jnp.sum(centred * weight, axis=1, keepdims=True)
    scores_ref[...] = jnp.broadcast_to(scores, (imps, 128)).T[:1]
    labels = jnp.broadcast_to(labels_ref[...].astype(F32), (8, imps)).T[:, :1]
    score_grad = 1.0 / (1.0 + jnp.exp(-scores)) - labels
    flat = weight - jnp.sum(weight, axis=1, keepdims=True) * (1.0 / columns)
    summed_grad = (score_grad * scale) * (flat - centred * (scale * scores * (1.0 / columns)))
    hidden_grad = rows_by_rows(summed_grad.astype(BF16), w_back_ref[...])
    pre_grad = (hidden_grad * slope).astype(BF16)
    cross_grad = (summed_grad * lifted).astype(BF16)
    joined_grad = (
        summed_grad * (1.0 + cross)
        + rows_by_rows(pre_grad, w_hidden_ref[...])
        + rows_by_rows(cross_grad, w_cross_ref[...])
    )
    item_grad_ref[...] = joined_grad[:, width:]
    user_part = joined_grad[:, :width].astype(BF16)
    per_user_ref[...] = jnp.dot(picks_t, user_part, preferred_element_type=F32).astype(BF16)


def finish_kernel(parts_ref, item_ref, scores_ref, pooled_ref, user_hbm, item_hbm, scores_hbm, pooled_hbm, sums_ref, sems):
    copies = [
        pltpu.make_async_copy(item_ref, item_hbm, sems.at[0]),
        pltpu.make_async_copy(scores_ref, scores_hbm, sems.at[1]),
        pltpu.make_async_copy(pooled_ref, pooled_hbm, sems.at[2]),
    ]
    for copy in copies:
        copy.start()
    sums_ref[...] = jnp.sum(parts_ref[...].astype(F32), axis=0)
    copies.append(pltpu.make_async_copy(sums_ref, user_hbm, sems.at[3]))
    copies[-1].start()
    for copy in copies:
        copy.wait()


HBM = pl.BlockSpec(memory_space=pltpu.HBM)
VMEM = pl.BlockSpec(memory_space=pltpu.VMEM)


def kernel_call(kernel, out_shape, flops, in_specs=None, out_specs=None, scratch=()):
    specs = {}
    if in_specs is not None:
        specs["in_specs"] = in_specs
    if out_specs is not None:
        specs["out_specs"] = out_specs
    return pl.pallas_call(
        kernel,
        out_shape=out_shape,
        scratch_shapes=list(scratch),
        compiler_params=pltpu.CompilerParams(vmem_limit_bytes=VMEM_LIMIT),
        cost_estimate=pl.CostEstimate(flops=flops, bytes_accessed=1 << 21, transcendentals=0),
        **specs,
    )


def body(
    hist_ids,
    hist_lens,
    table_rows,
    imp_user,
    item_rows,
    labels,
    w_hidden,
    b_hidden,
    w_back,
    w_cross,
    b_cross,
    norm_gain,
    w_score,
):
    users, sources, slots = hist_ids.shape
    table_count, width = table_rows.shape
    samples = lax.axis_size("sample")
    imps = imp_user.shape[0]
    history = slots * sources * 2 // 3
    like = lambda array: jax.ShapeDtypeStruct(array.shape, array.dtype)
    row = lambda vector: vector.reshape(1, -1)
    chips = sources // 2
    sides = [[2 * chip + core for chip in range(chips)] for core in range(2)]
    other_rows = lax.ppermute(table_rows, "table", [(i, i ^ 1) for i in range(sources)])
    with jax.named_scope("pack_ids"):
        words = pack_words(jnp.transpose(hist_ids, (0, 2, 1)), hist_lens)
        words = kernel_call(
            turn_kernel,
            jax.ShapeDtypeStruct((chips, 2, users * slots // 2), jnp.int32),
            1 << 34,
        )(words)
    words = lax.all_to_all(
        words, "table", split_axis=0, concat_axis=0, tiled=True, axis_index_groups=sides
    )
    vectors = tuple(map(row, (imp_user, labels, b_hidden, b_cross, norm_gain, w_score)))
    with jax.named_scope("pool"):
        partials, *vectors = kernel_call(
            lambda *refs: pool_kernel(users, len(vectors), *refs),
            (jax.ShapeDtypeStruct((chips, users, width), BF16),) + tuple(map(like, vectors)),
            1 << 33,
            in_specs=[VMEM, VMEM] + [HBM] * (1 + len(vectors)),
            scratch=[
                pltpu.VMEM((2 * (table_count // LOW), chips * users, LOW), BF16),
                pltpu.VMEM((table_count, width), BF16),
                pltpu.SemaphoreType.DMA((1 + len(vectors),)),
            ],
        )(words, other_rows, table_rows, *vectors)
    imp_row, label_row, b_hidden, b_cross, norm_gain, w_score = vectors
    returned = lax.all_to_all(
        partials, "table", split_axis=0, concat_axis=0, tiled=True, axis_index_groups=sides
    )
    pooled_user = (jnp.sum(returned.astype(F32), axis=0) * float(history) ** (-0.5)).astype(BF16)
    group_rows = lax.all_to_all(
        jnp.broadcast_to(pooled_user[None], (samples, users, width)),
        "sample",
        split_axis=0,
        concat_axis=0,
        tiled=True,
    ).reshape(samples * users, width)
    with jax.named_scope("dense"):
        scores, item_grad, per_user = kernel_call(
            dense_kernel,
            (
                jax.ShapeDtypeStruct((1, imps), F32),
                jax.ShapeDtypeStruct((imps, width), F32),
                jax.ShapeDtypeStruct((samples * users, width), BF16),
            ),
            1 << 30,
        )(
            group_rows,
            imp_row,
            item_rows,
            label_row,
            w_hidden,
            b_hidden,
            w_back,
            w_cross,
            b_cross,
            norm_gain,
            w_score,
        )
    parts = lax.all_to_all(
        per_user.reshape(samples, users, width), "sample", split_axis=0, concat_axis=0, tiled=True
    )
    with jax.named_scope("finish"):
        user_grad, item_grad, scores, pooled_user = kernel_call(
            finish_kernel,
            (jax.ShapeDtypeStruct((users, width), F32), like(item_grad), like(scores), like(pooled_user)),
            1 << 20,
            in_specs=[VMEM] * 4,
            out_specs=[HBM] * 4,
            scratch=[pltpu.VMEM((users, width), F32), pltpu.SemaphoreType.DMA((4,))],
        )(parts, item_grad, scores, pooled_user)
    return (pooled_user, scores.reshape(-1), user_grad, item_grad)


def solution(mesh):
    both = ("table", "sample")
    in_specs = (
        P(both, None, None),
        P(both, None),
        P("table", None),
        P(both),
        P(both, None),
        P(both),
    ) + (P(),) * 7
    out_specs = (P(both, None), P(both), P(both, None), P(both, None))
    return jax.shard_map(body, mesh=mesh, in_specs=in_specs, out_specs=out_specs, check_vma=False)
```

```python
import jax
import jax.numpy as jnp
from jax import lax
from jax.experimental import pallas as pl
from jax.experimental.pallas import tpu as pltpu
from jax.sharding import PartitionSpec as P

F32 = jnp.float32
BF16 = jnp.bfloat16
F8 = jnp.float8_e4m3fn
LOW = 256
VMEM_LIMIT = 32 * 1024 * 1024


def rows_by_rows(a, b):
    return lax.dot_general(a, b, (((1,), (1,)), ((), ())), preferred_element_type=F32)


def pack_words(ids, lens):
    live = lax.broadcasted_iota(jnp.int32, ids.shape, 1) < lens[:, None, :]
    ids = jnp.where(live, ids, -1)
    half = ids.shape[0] // 2
    return (ids[:half] & 0xFFFF) | (ids[half:] << 16)


def turn_kernel(words_ref, out_ref):
    half, slots, shards = words_ref.shape
    words = words_ref[...].reshape(half * slots, shards).T
    chips, cores, _ = out_ref.shape
    for chip in range(chips):
        out_ref[chip] = words[chip * cores : (chip + 1) * cores]


def count_kernel(users, n_staged, words_ref, *refs):
    staged, (counts_ref, *staged_refs) = refs[:n_staged], refs[n_staged:]
    for source_ref, target_ref in zip(staged, staged_refs):
        target_ref[...] = source_ref[...]
    sources = words_ref.shape[0]
    first_core = lax.rem(lax.axis_index("table"), 2) == 0
    positions = 2 * words_ref.shape[2]
    highs = counts_ref.shape[0] // 2
    slots = positions // users
    user_of = lax.broadcasted_iota(jnp.int32, (1, positions), 1) // slots
    high_rows = lax.broadcasted_iota(jnp.int32, (highs * users, positions), 0).astype(jnp.int8)
    low_rows = (lax.broadcasted_iota(jnp.int32, (LOW, positions), 0) - LOW // 2).astype(jnp.int8)
    one, zero = jnp.ones((), F8), jnp.zeros((), F8)

    def count(source, carry):
        pair = words_ref[source]
        own = jnp.where(first_core, pair[:1], pair[1:])
        other = jnp.where(first_core, pair[1:], pair[:1])
        rows = pl.ds(pl.multiple_of(source * users, users), users)
        for shard, words in enumerate((own, other)):
            ids = jnp.concatenate([words & 0xFFFF, (words >> 16) & 0xFFFF], axis=1)
            high = (ids // LOW) * users + user_of
            high = jnp.where(high < highs * users, high, -1).astype(jnp.int8)
            low = (ids % LOW - LOW // 2).astype(jnp.int8)
            high_hot = jnp.where(high == high_rows, one, zero)
            low_hot = jnp.where(low == low_rows, one, zero)
            counts = rows_by_rows(high_hot, low_hot).astype(BF16)
            for part in range(highs):
                counts_ref[shard * highs + part, rows, :] = counts[part * users : (part + 1) * users]
        return carry

    lax.fori_loop(0, sources, count, 0, unroll=32)


def pool_kernel(counts_ref, own_ref, other_ref, out_ref):
    parts = counts_ref.shape[0]
    sources, users, width = out_ref.shape
    chunk = 16
    for first in range(0, sources, chunk):
        total = None
        for part in range(parts):
            shard_ref = (own_ref, other_ref)[part // (parts // 2)]
            low_row = part % (parts // 2) * LOW
            term = jnp.dot(
                counts_ref[part, first * users : (first + chunk) * users, :],
                shard_ref[low_row : low_row + LOW, :],
                preferred_element_type=F32,
            )
            total = term if total is None else total + term
        out_ref[first : first + chunk] = total.astype(BF16).reshape(chunk, users, width)


def dense_kernel(
    rows_ref,
    imp_ref,
    item_ref,
    labels_ref,
    w_hidden_ref,
    b_hidden_ref,
    w_back_ref,
    w_cross_ref,
    b_cross_ref,
    gain_ref,
    w_score_ref,
    scores_ref,
    item_grad_ref,
    per_user_ref,
):
    group_users, width = rows_ref.shape
    imps = item_ref.shape[0]
    picks_t = jnp.where(
        lax.broadcasted_iota(jnp.int32, (group_users, imps), 0) == imp_ref[...], 1.0, 0.0
    ).astype(F32)
    picks = picks_t.T.astype(BF16)
    picks_t = picks_t.astype(BF16)
    user_feat = jnp.dot(picks, rows_ref[...], preferred_element_type=F32).astype(BF16)
    joined = jnp.concatenate([user_feat, item_ref[...]], axis=1)
    lifted = joined.astype(F32)
    pre = jnp.dot(joined, w_hidden_ref[...], preferred_element_type=F32) + b_hidden_ref[...]
    cross = jnp.dot(joined, w_cross_ref[...], preferred_element_type=F32) + b_cross_ref[...]
    k, c = 0.7978845608028654, 0.044715
    square = pre * pre
    tanh = jnp.tanh(k * pre * (1.0 + c * square))
    cdf = 0.5 * (1.0 + tanh)
    hidden = (pre * cdf).astype(BF16)
    slope = cdf + 0.5 * pre * (1.0 - tanh * tanh) * (k * (1.0 + 3.0 * c * square))
    summed = lifted + jnp.dot(hidden, w_back_ref[...], preferred_element_type=F32) + lifted * cross
    columns = summed.shape[1]
    centred = summed - jnp.sum(summed, axis=1, keepdims=True) * (1.0 / columns)
    variance = jnp.sum(centred * centred, axis=1, keepdims=True) * (1.0 / columns)
    scale = lax.rsqrt(variance + 1e-05)
    weight = gain_ref[...] * w_score_ref[...]
    scores = scale * jnp.sum(centred * weight, axis=1, keepdims=True)
    scores_ref[...] = jnp.broadcast_to(scores, (imps, 128)).T[:1]
    labels = jnp.broadcast_to(labels_ref[...].astype(F32), (8, imps)).T[:, :1]
    score_grad = 1.0 / (1.0 + jnp.exp(-scores)) - labels
    flat = weight - jnp.sum(weight, axis=1, keepdims=True) * (1.0 / columns)
    summed_grad = (score_grad * scale) * (flat - centred * (scale * scores * (1.0 / columns)))
    hidden_grad = rows_by_rows(summed_grad.astype(BF16), w_back_ref[...])
    pre_grad = (hidden_grad * slope).astype(BF16)
    cross_grad = (summed_grad * lifted).astype(BF16)
    joined_grad = (
        summed_grad * (1.0 + cross)
        + rows_by_rows(pre_grad, w_hidden_ref[...])
        + rows_by_rows(cross_grad, w_cross_ref[...])
    )
    item_grad_ref[...] = joined_grad[:, width:]
    user_part = joined_grad[:, :width].astype(BF16)
    per_user_ref[...] = jnp.dot(picks_t, user_part, preferred_element_type=F32).astype(BF16)


def finish_kernel(parts_ref, item_ref, scores_ref, pooled_ref, user_hbm, item_hbm, scores_hbm, pooled_hbm, sums_ref, sems):
    copies = [
        pltpu.make_async_copy(item_ref, item_hbm, sems.at[0]),
        pltpu.make_async_copy(scores_ref, scores_hbm, sems.at[1]),
        pltpu.make_async_copy(pooled_ref, pooled_hbm, sems.at[2]),
    ]
    for copy in copies:
        copy.start()
    sums_ref[...] = jnp.sum(parts_ref[...].astype(F32), axis=0)
    copies.append(pltpu.make_async_copy(sums_ref, user_hbm, sems.at[3]))
    copies[-1].start()
    for copy in copies:
        copy.wait()


HBM = pl.BlockSpec(memory_space=pltpu.HBM)
VMEM = pl.BlockSpec(memory_space=pltpu.VMEM)


def kernel_call(kernel, out_shape, flops, in_specs=None, out_specs=None, scratch=()):
    specs = {}
    if in_specs is not None:
        specs["in_specs"] = in_specs
    if out_specs is not None:
        specs["out_specs"] = out_specs
    return pl.pallas_call(
        kernel,
        out_shape=out_shape,
        scratch_shapes=list(scratch),
        compiler_params=pltpu.CompilerParams(vmem_limit_bytes=VMEM_LIMIT),
        cost_estimate=pl.CostEstimate(flops=flops, bytes_accessed=1 << 21, transcendentals=0),
        **specs,
    )


def body(
    hist_ids,
    hist_lens,
    table_rows,
    imp_user,
    item_rows,
    labels,
    w_hidden,
    b_hidden,
    w_back,
    w_cross,
    b_cross,
    norm_gain,
    w_score,
):
    users, sources, slots = hist_ids.shape
    table_count, width = table_rows.shape
    samples = lax.axis_size("sample")
    imps = imp_user.shape[0]
    history = slots * sources * 2 // 3
    like = lambda array: jax.ShapeDtypeStruct(array.shape, array.dtype)
    row = lambda vector: vector.reshape(1, -1)
    chips = sources // 2
    sides = [[2 * chip + core for chip in range(chips)] for core in range(2)]
    with jax.named_scope("pack_ids"):
        words = pack_words(jnp.transpose(hist_ids, (0, 2, 1)), hist_lens)
        words = kernel_call(
            turn_kernel,
            jax.ShapeDtypeStruct((chips, 2, users * slots // 2), jnp.int32),
            1 << 34,
        )(words)
    other_rows = lax.ppermute(table_rows, "table", [(i, i ^ 1) for i in range(sources)])
    words = lax.all_to_all(
        words, "table", split_axis=0, concat_axis=0, tiled=True, axis_index_groups=sides
    )
    vectors = tuple(map(row, (imp_user, labels, b_hidden, b_cross, norm_gain, w_score)))
    with jax.named_scope("count"):
        counts, *vectors = kernel_call(
            lambda *refs: count_kernel(users, len(vectors), *refs),
            (jax.ShapeDtypeStruct((2 * (table_count // LOW), chips * users, LOW), BF16),)
            + tuple(map(like, vectors)),
            1 << 33,
        )(words, *vectors)
    with jax.named_scope("pool"):
        partials = kernel_call(
            pool_kernel, jax.ShapeDtypeStruct((chips, users, width), BF16), 1 << 30
        )(counts, table_rows, other_rows)
    imp_row, label_row, b_hidden, b_cross, norm_gain, w_score = vectors
    returned = lax.all_to_all(
        partials, "table", split_axis=0, concat_axis=0, tiled=True, axis_index_groups=sides
    )
    pooled_user = (jnp.sum(returned.astype(F32), axis=0) * float(history) ** (-0.5)).astype(BF16)
    group_rows = lax.all_to_all(
        jnp.broadcast_to(pooled_user[None], (samples, users, width)),
        "sample",
        split_axis=0,
        concat_axis=0,
        tiled=True,
    ).reshape(samples * users, width)
    with jax.named_scope("dense"):
        scores, item_grad, per_user = kernel_call(
            dense_kernel,
            (
                jax.ShapeDtypeStruct((1, imps), F32),
                jax.ShapeDtypeStruct((imps, width), F32),
                jax.ShapeDtypeStruct((samples * users, width), BF16),
            ),
            1 << 30,
        )(
            group_rows,
            imp_row,
            item_rows,
            label_row,
            w_hidden,
            b_hidden,
            w_back,
            w_cross,
            b_cross,
            norm_gain,
            w_score,
        )
    parts = lax.all_to_all(
        per_user.reshape(samples, users, width), "sample", split_axis=0, concat_axis=0, tiled=True
    )
    with jax.named_scope("finish"):
        user_grad, item_grad, scores, pooled_user = kernel_call(
            finish_kernel,
            (jax.ShapeDtypeStruct((users, width), F32), like(item_grad), like(scores), like(pooled_user)),
            1 << 20,
            in_specs=[VMEM] * 4,
            out_specs=[HBM] * 4,
            scratch=[pltpu.VMEM((users, width), F32), pltpu.SemaphoreType.DMA((4,))],
        )(parts, item_grad, scores, pooled_user)
    return (pooled_user, scores.reshape(-1), user_grad, item_grad)


def solution(mesh):
    both = ("table", "sample")
    in_specs = (
        P(both, None, None),
        P(both, None),
        P("table", None),
        P(both),
        P(both, None),
        P(both),
    ) + (P(),) * 7
    out_specs = (P(both, None), P(both), P(both, None), P(both, None))
    return jax.shard_map(body, mesh=mesh, in_specs=in_specs, out_specs=out_specs, check_vma=False)
```

```python
import jax
import jax.numpy as jnp
from jax import lax
from jax.experimental import pallas as pl
from jax.experimental.pallas import tpu as pltpu
from jax.sharding import PartitionSpec as P

F32 = jnp.float32
BF16 = jnp.bfloat16
F8 = jnp.float8_e4m3fn
LOW_BITS = 7
LOW = 1 << LOW_BITS
DEPTH = 256
HALF = 8
VMEM_LIMIT = 32 * 1024 * 1024


def rows_by_rows(a, b):
    return lax.dot_general(a, b, (((1,), (1,)), ((), ())), preferred_element_type=F32)


def pack_words(ids, lens):
    live = lax.broadcasted_iota(jnp.int32, ids.shape, 1) < lens[:, None, :]
    ids = jnp.where(live, ids, -1)
    half = ids.shape[0] // 2
    return (ids[:half] & 0xFFFF) | (ids[half:] << 16)


def turn_kernel(words_ref, out_ref):
    half, slots, shards = words_ref.shape
    words = words_ref[...].reshape(half * slots, shards).T
    chips, cores, _ = out_ref.shape
    for chip in range(chips):
        out_ref[chip] = words[chip * cores : (chip + 1) * cores]


def count_kernel(users, words_ref, *refs):
    counts_ref = refs[-1]
    sources = words_ref.shape[0]
    first_core = lax.rem(lax.axis_index("table"), 2) == 0
    positions = 2 * words_ref.shape[2]
    slots = positions // users
    side_by_side = counts_ref.shape[2] // LOW
    highs = counts_ref.shape[0] // 2 * side_by_side
    low_rows = lax.broadcasted_iota(jnp.int32, (LOW, positions), 0).astype(jnp.int8)
    one, zero = jnp.ones((), F8), jnp.zeros((), F8)
    tiles = []
    for first in range(0, positions, DEPTH):
        groups = sorted({first // slots // HALF, (first + DEPTH - 1) // slots // HALF})
        rows = len(groups) * HALF
        middle = highs * rows // 2
        user = (lax.broadcasted_iota(jnp.int32, (1, DEPTH), 1) + first) // slots - groups[0] * HALF
        code_rows = lax.broadcasted_iota(jnp.int32, (highs * rows, DEPTH), 0) - middle
        tiles.append((slice(first, first + DEPTH), groups, rows, user - middle, code_rows.astype(jnp.int8)))

    def count(source, carry):
        pair = words_ref[source]
        own = jnp.where(first_core, pair[:1], pair[1:])
        other = jnp.where(first_core, pair[1:], pair[:1])
        target = pl.ds(pl.multiple_of(source * users, users), users)
        for shard, words in enumerate((own, other)):
            ids = jnp.concatenate([words & 0xFFFF, (words >> 16) & 0xFFFF], axis=1)
            low = jnp.where(ids < highs * LOW, ids & (LOW - 1), -1).astype(jnp.int8)
            high = (ids >> LOW_BITS) & (highs - 1)
            low_hot = jnp.where(low == low_rows, one, zero)
            found = {}
            for piece, groups, rows, base, code_rows in tiles:
                code = (high[:, piece] * rows + base).astype(jnp.int8)
                high_hot = jnp.where(code == code_rows, one, zero)
                counts = rows_by_rows(high_hot, low_hot[:, piece])
                for part in range(highs):
                    for i, group in enumerate(groups):
                        start = part * rows + i * HALF
                        found.setdefault((part, group), []).append(counts[start : start + HALF])
            for part in range(highs):
                sums = [sum(found[part, group][1:], found[part, group][0]) for group in range(users // HALF)]
                lane = part % side_by_side * LOW
                counts_ref[(shard * highs + part) // side_by_side, target, lane : lane + LOW] = jnp.concatenate(
                    sums, axis=0
                ).astype(BF16)
        return carry

    lax.fori_loop(0, sources, count, 0, unroll=32)


def pool_kernel(counts_ref, own_ref, other_ref, out_ref):
    parts, _, depth = counts_ref.shape
    sources, users, width = out_ref.shape
    chunk = 16
    for first in range(0, sources, chunk):
        total = None
        for part in range(parts):
            shard_ref = (own_ref, other_ref)[part // (parts // 2)]
            low_row = part % (parts // 2) * depth
            term = jnp.dot(
                counts_ref[part, first * users : (first + chunk) * users, :],
                shard_ref[low_row : low_row + depth, :],
                preferred_element_type=F32,
            )
            total = term if total is None else total + term
        out_ref[first : first + chunk] = total.astype(BF16).reshape(chunk, users, width)


def dense_kernel(
    rows_ref,
    imp_ref,
    item_ref,
    labels_ref,
    w_hidden_ref,
    b_hidden_ref,
    w_back_ref,
    w_cross_ref,
    b_cross_ref,
    gain_ref,
    w_score_ref,
    scores_ref,
    item_grad_ref,
    per_user_ref,
):
    group_users, width = rows_ref.shape
    imps = item_ref.shape[0]
    picks_t = jnp.where(
        lax.broadcasted_iota(jnp.int32, (group_users, imps), 0) == imp_ref[...], 1.0, 0.0
    ).astype(F32)
    picks = picks_t.T.astype(BF16)
    picks_t = picks_t.astype(BF16)
    user_feat = jnp.dot(picks, rows_ref[...], preferred_element_type=F32).astype(BF16)
    joined = jnp.concatenate([user_feat, item_ref[...]], axis=1)
    lifted = joined.astype(F32)
    pre = jnp.dot(joined, w_hidden_ref[...], preferred_element_type=F32) + b_hidden_ref[...]
    factor = jnp.dot(joined, w_cross_ref[...], preferred_element_type=F32) + (b_cross_ref[...] + 1.0)
    k, c = 0.7978845608028654, 0.044715
    square = pre * pre
    half_tanh = 0.5 * jnp.tanh(pre * (k + (k * c) * square))
    cdf = 0.5 + half_tanh
    hidden = (pre * cdf).astype(BF16)
    slope = cdf + (cdf * (0.5 - half_tanh)) * (pre * (2.0 * k + (6.0 * k * c) * square))
    summed = jnp.dot(hidden, w_back_ref[...], preferred_element_type=F32) + lifted * factor
    columns = summed.shape[1]
    centred = summed - jnp.sum(summed, axis=1, keepdims=True) * (1.0 / columns)
    variance = jnp.sum(centred * centred, axis=1, keepdims=True) * (1.0 / columns)
    scale = lax.rsqrt(variance + 1e-05)
    weight = gain_ref[...] * w_score_ref[...]
    scores = scale * jnp.sum(centred * weight, axis=1, keepdims=True)
    scores_ref[...] = jnp.broadcast_to(scores, (imps, 128)).T[:1]
    labels = jnp.broadcast_to(labels_ref[...].astype(F32), (8, imps)).T[:, :1]
    score_grad = 1.0 / (1.0 + jnp.exp(-scores)) - labels
    flat = weight - jnp.sum(weight, axis=1, keepdims=True) * (1.0 / columns)
    summed_grad = (score_grad * scale) * (flat - centred * (scale * scores * (1.0 / columns)))
    hidden_grad = rows_by_rows(summed_grad.astype(BF16), w_back_ref[...])
    pre_grad = (hidden_grad * slope).astype(BF16)
    cross_grad = (summed_grad * lifted).astype(BF16)
    joined_grad = (
        summed_grad * factor
        + rows_by_rows(pre_grad, w_hidden_ref[...])
        + rows_by_rows(cross_grad, w_cross_ref[...])
    )
    item_grad_ref[...] = joined_grad[:, width:]
    user_part = joined_grad[:, :width].astype(BF16)
    per_user_ref[...] = jnp.dot(picks_t, user_part, preferred_element_type=F32).astype(BF16)


def finish_kernel(parts_ref, item_ref, scores_ref, pooled_ref, user_hbm, item_hbm, scores_hbm, pooled_hbm, sums_ref, sems):
    copies = [
        pltpu.make_async_copy(item_ref, item_hbm, sems.at[0]),
        pltpu.make_async_copy(scores_ref, scores_hbm, sems.at[1]),
        pltpu.make_async_copy(pooled_ref, pooled_hbm, sems.at[2]),
    ]
    for copy in copies:
        copy.start()
    sums_ref[...] = jnp.sum(parts_ref[...].astype(F32), axis=0)
    copies.append(pltpu.make_async_copy(sums_ref, user_hbm, sems.at[3]))
    copies[-1].start()
    for copy in copies:
        copy.wait()


HBM = pl.BlockSpec(memory_space=pltpu.HBM)
VMEM = pl.BlockSpec(memory_space=pltpu.VMEM)


def kernel_call(kernel, out_shape, flops, in_specs=None, out_specs=None, scratch=()):
    specs = {}
    if in_specs is not None:
        specs["in_specs"] = in_specs
    if out_specs is not None:
        specs["out_specs"] = out_specs
    return pl.pallas_call(
        kernel,
        out_shape=out_shape,
        scratch_shapes=list(scratch),
        compiler_params=pltpu.CompilerParams(vmem_limit_bytes=VMEM_LIMIT),
        cost_estimate=pl.CostEstimate(flops=flops, bytes_accessed=1 << 21, transcendentals=0),
        **specs,
    )


def body(
    hist_ids,
    hist_lens,
    table_rows,
    imp_user,
    item_rows,
    labels,
    w_hidden,
    b_hidden,
    w_back,
    w_cross,
    b_cross,
    norm_gain,
    w_score,
):
    users, sources, slots = hist_ids.shape
    table_count, width = table_rows.shape
    samples = lax.axis_size("sample")
    imps = imp_user.shape[0]
    history = slots * sources * 2 // 3
    like = lambda array: jax.ShapeDtypeStruct(array.shape, array.dtype)
    row = lambda vector: vector.reshape(1, -1)
    chips = sources // 2
    sides = [[2 * chip + core for chip in range(chips)] for core in range(2)]
    with jax.named_scope("pack_ids"):
        words = pack_words(jnp.transpose(hist_ids, (0, 2, 1)), hist_lens)
        words = kernel_call(
            turn_kernel,
            jax.ShapeDtypeStruct((chips, 2, users * slots // 2), jnp.int32),
            1 << 34,
        )(words)
    other_rows = lax.ppermute(table_rows, "table", [(i, i ^ 1) for i in range(sources)])
    words = lax.all_to_all(
        words, "table", split_axis=0, concat_axis=0, tiled=True, axis_index_groups=sides
    )
    vectors = tuple(map(row, (imp_user, labels, b_hidden, b_cross, norm_gain, w_score)))
    with jax.named_scope("count"):
        counts = kernel_call(
            lambda *refs: count_kernel(users, *refs),
            jax.ShapeDtypeStruct((2 * (table_count // DEPTH), chips * users, DEPTH), BF16),
            1 << 33,
        )(words, *vectors)
    with jax.named_scope("pool"):
        partials = kernel_call(
            pool_kernel, jax.ShapeDtypeStruct((chips, users, width), BF16), 1 << 30
        )(counts, table_rows, other_rows)
    imp_row, label_row, b_hidden, b_cross, norm_gain, w_score = vectors
    returned = lax.all_to_all(
        partials, "table", split_axis=0, concat_axis=0, tiled=True, axis_index_groups=sides
    )
    pooled_user = (jnp.sum(returned.astype(F32), axis=0) * float(history) ** (-0.5)).astype(BF16)
    group_rows = lax.all_to_all(
        jnp.broadcast_to(pooled_user[None], (samples, users, width)),
        "sample",
        split_axis=0,
        concat_axis=0,
        tiled=True,
    ).reshape(samples * users, width)
    with jax.named_scope("dense"):
        scores, item_grad, per_user = kernel_call(
            dense_kernel,
            (
                jax.ShapeDtypeStruct((1, imps), F32),
                jax.ShapeDtypeStruct((imps, width), F32),
                jax.ShapeDtypeStruct((samples * users, width), BF16),
            ),
            1 << 30,
        )(
            group_rows,
            imp_row,
            item_rows,
            label_row,
            w_hidden,
            b_hidden,
            w_back,
            w_cross,
            b_cross,
            norm_gain,
            w_score,
        )
    parts = lax.all_to_all(
        per_user.reshape(samples, users, width), "sample", split_axis=0, concat_axis=0, tiled=True
    )
    with jax.named_scope("finish"):
        user_grad, item_grad, scores, pooled_user = kernel_call(
            finish_kernel,
            (jax.ShapeDtypeStruct((users, width), F32), like(item_grad), like(scores), like(pooled_user)),
            1 << 20,
            in_specs=[VMEM] * 4,
            out_specs=[HBM] * 4,
            scratch=[pltpu.VMEM((users, width), F32), pltpu.SemaphoreType.DMA((4,))],
        )(parts, item_grad, scores, pooled_user)
    return (pooled_user, scores.reshape(-1), user_grad, item_grad)


def solution(mesh):
    both = ("table", "sample")
    in_specs = (
        P(both, None, None),
        P(both, None),
        P("table", None),
        P(both),
        P(both, None),
        P(both),
    ) + (P(),) * 7
    out_specs = (P(both, None), P(both), P(both, None), P(both, None))
    return jax.shard_map(body, mesh=mesh, in_specs=in_specs, out_specs=out_specs, check_vma=False)
```

```python
import jax
import jax.numpy as jnp
from jax import lax
from jax.experimental import pallas as pl
from jax.experimental.pallas import tpu as pltpu
from jax.sharding import PartitionSpec as P

F32 = jnp.float32
BF16 = jnp.bfloat16
F8 = jnp.float8_e4m3fn
LOW_BITS = 7
LOW = 1 << LOW_BITS
DEPTH = 256
VMEM_LIMIT = 32 * 1024 * 1024


def rows_by_rows(a, b):
    return lax.dot_general(a, b, (((1,), (1,)), ((), ())), preferred_element_type=F32)


def pack_words(ids, lens):
    live = lax.broadcasted_iota(jnp.int32, ids.shape, 1) < lens[:, None, :]
    ids = jnp.where(live, ids, -1)
    half = ids.shape[0] // 2
    return (ids[:half] & 0xFFFF) | (ids[half:] << 16)


def turn_kernel(words_ref, out_ref):
    half, slots, shards = words_ref.shape
    words = words_ref[...].reshape(half * slots, shards).T
    chips, cores, _ = out_ref.shape
    for chip in range(chips):
        out_ref[chip] = words[chip * cores : (chip + 1) * cores]


def count_kernel(users, words_ref, *refs):
    counts_ref = refs[-1]
    sources, _, positions = words_ref.shape
    half = users // 2
    side_by_side = counts_ref.shape[2] // LOW
    highs = counts_ref.shape[0] // 2 * side_by_side
    first_core = lax.rem(lax.axis_index("table"), 2) == 0
    user_of = lax.broadcasted_iota(jnp.int32, (1, positions), 1) // (positions // half)
    high_rows = lax.broadcasted_iota(jnp.int32, (highs * half, positions), 0).astype(jnp.int8)
    low_rows = lax.broadcasted_iota(jnp.int32, (LOW, positions), 0).astype(jnp.int8)
    one, zero = jnp.ones((), F8), jnp.zeros((), F8)

    def count(source, carry):
        pair = words_ref[source]
        own = jnp.where(first_core, pair[:1], pair[1:])
        other = jnp.where(first_core, pair[1:], pair[:1])
        target = pl.ds(pl.multiple_of(source * users, users), users)
        for shard, words in enumerate((own, other)):
            halves = []
            for ids in (words & 0xFFFF, (words >> 16) & 0xFFFF):
                low = jnp.where(ids < highs * LOW, ids & (LOW - 1), -1).astype(jnp.int8)
                high = (((ids >> LOW_BITS) & (highs - 1)) * half + user_of).astype(jnp.int8)
                high_hot = jnp.where(high == high_rows, one, zero)
                low_hot = jnp.where(low == low_rows, one, zero)
                halves.append(rows_by_rows(high_hot, low_hot))
            for part in range(highs):
                rows = slice(part * half, (part + 1) * half)
                lane = part % side_by_side * LOW
                counts_ref[(shard * highs + part) // side_by_side, target, lane : lane + LOW] = jnp.concatenate(
                    [counts[rows] for counts in halves], axis=0
                ).astype(BF16)
        return carry

    lax.fori_loop(0, sources, count, 0, unroll=32)


def pool_kernel(counts_ref, own_ref, other_ref, out_ref):
    parts, _, depth = counts_ref.shape
    sources, users, width = out_ref.shape
    chunk = 16
    for first in range(0, sources, chunk):
        total = None
        for part in range(parts):
            shard_ref = (own_ref, other_ref)[part // (parts // 2)]
            low_row = part % (parts // 2) * depth
            term = jnp.dot(
                counts_ref[part, first * users : (first + chunk) * users, :],
                shard_ref[low_row : low_row + depth, :],
                preferred_element_type=F32,
            )
            total = term if total is None else total + term
        out_ref[first : first + chunk] = total.astype(BF16).reshape(chunk, users, width)


def dense_kernel(
    rows_ref,
    imp_ref,
    item_ref,
    labels_ref,
    w_hidden_ref,
    b_hidden_ref,
    w_back_ref,
    w_cross_ref,
    b_cross_ref,
    gain_ref,
    w_score_ref,
    scores_ref,
    item_grad_ref,
    per_user_ref,
):
    group_users, width = rows_ref.shape
    imps = item_ref.shape[0]
    picks_t = jnp.where(
        lax.broadcasted_iota(jnp.int32, (group_users, imps), 0) == imp_ref[...], 1.0, 0.0
    ).astype(F32)
    picks = picks_t.T.astype(BF16)
    picks_t = picks_t.astype(BF16)
    user_feat = jnp.dot(picks, rows_ref[...], preferred_element_type=F32).astype(BF16)
    joined = jnp.concatenate([user_feat, item_ref[...]], axis=1)
    lifted = joined.astype(F32)
    pre = jnp.dot(joined, w_hidden_ref[...], preferred_element_type=F32) + b_hidden_ref[...]
    factor = jnp.dot(joined, w_cross_ref[...], preferred_element_type=F32) + (b_cross_ref[...] + 1.0)
    k, c = 0.7978845608028654, 0.044715
    square = pre * pre
    half_tanh = 0.5 * jnp.tanh(pre * (k + (k * c) * square))
    cdf = 0.5 + half_tanh
    hidden = (pre * cdf).astype(BF16)
    slope = cdf + (cdf * (0.5 - half_tanh)) * (pre * (2.0 * k + (6.0 * k * c) * square))
    summed = jnp.dot(hidden, w_back_ref[...], preferred_element_type=F32) + lifted * factor
    columns = summed.shape[1]
    centred = summed - jnp.sum(summed, axis=1, keepdims=True) * (1.0 / columns)
    variance = jnp.sum(centred * centred, axis=1, keepdims=True) * (1.0 / columns)
    scale = lax.rsqrt(variance + 1e-05)
    weight = gain_ref[...] * w_score_ref[...]
    scores = scale * jnp.sum(centred * weight, axis=1, keepdims=True)
    scores_ref[...] = jnp.broadcast_to(scores, (imps, 128)).T[:1]
    labels = jnp.broadcast_to(labels_ref[...].astype(F32), (8, imps)).T[:, :1]
    score_grad = 1.0 / (1.0 + jnp.exp(-scores)) - labels
    flat = weight - jnp.sum(weight, axis=1, keepdims=True) * (1.0 / columns)
    summed_grad = (score_grad * scale) * (flat - centred * (scale * scores * (1.0 / columns)))
    hidden_grad = rows_by_rows(summed_grad.astype(BF16), w_back_ref[...])
    pre_grad = (hidden_grad * slope).astype(BF16)
    cross_grad = (summed_grad * lifted).astype(BF16)
    joined_grad = (
        summed_grad * factor
        + rows_by_rows(pre_grad, w_hidden_ref[...])
        + rows_by_rows(cross_grad, w_cross_ref[...])
    )
    item_grad_ref[...] = joined_grad[:, width:]
    user_part = joined_grad[:, :width].astype(BF16)
    per_user_ref[...] = jnp.dot(picks_t, user_part, preferred_element_type=F32).astype(BF16)


def finish_kernel(parts_ref, item_ref, scores_ref, pooled_ref, user_hbm, item_hbm, scores_hbm, pooled_hbm, sums_ref, sems):
    copies = [
        pltpu.make_async_copy(item_ref, item_hbm, sems.at[0]),
        pltpu.make_async_copy(scores_ref, scores_hbm, sems.at[1]),
        pltpu.make_async_copy(pooled_ref, pooled_hbm, sems.at[2]),
    ]
    for copy in copies:
        copy.start()
    sums_ref[...] = jnp.sum(parts_ref[...].astype(F32), axis=0)
    copies.append(pltpu.make_async_copy(sums_ref, user_hbm, sems.at[3]))
    copies[-1].start()
    for copy in copies:
        copy.wait()


HBM = pl.BlockSpec(memory_space=pltpu.HBM)
VMEM = pl.BlockSpec(memory_space=pltpu.VMEM)


def kernel_call(kernel, out_shape, flops, in_specs=None, out_specs=None, scratch=()):
    specs = {}
    if in_specs is not None:
        specs["in_specs"] = in_specs
    if out_specs is not None:
        specs["out_specs"] = out_specs
    return pl.pallas_call(
        kernel,
        out_shape=out_shape,
        scratch_shapes=list(scratch),
        compiler_params=pltpu.CompilerParams(vmem_limit_bytes=VMEM_LIMIT),
        cost_estimate=pl.CostEstimate(flops=flops, bytes_accessed=1 << 21, transcendentals=0),
        **specs,
    )


def body(
    hist_ids,
    hist_lens,
    table_rows,
    imp_user,
    item_rows,
    labels,
    w_hidden,
    b_hidden,
    w_back,
    w_cross,
    b_cross,
    norm_gain,
    w_score,
):
    users, sources, slots = hist_ids.shape
    table_count, width = table_rows.shape
    samples = lax.axis_size("sample")
    imps = imp_user.shape[0]
    history = slots * sources * 2 // 3
    like = lambda array: jax.ShapeDtypeStruct(array.shape, array.dtype)
    row = lambda vector: vector.reshape(1, -1)
    chips = sources // 2
    sides = [[2 * chip + core for chip in range(chips)] for core in range(2)]
    with jax.named_scope("pack_ids"):
        words = pack_words(jnp.transpose(hist_ids, (0, 2, 1)), hist_lens)
        words = kernel_call(
            turn_kernel,
            jax.ShapeDtypeStruct((chips, 2, users * slots // 2), jnp.int32),
            1 << 34,
        )(words)
    other_rows = lax.ppermute(table_rows, "table", [(i, i ^ 1) for i in range(sources)])
    words = lax.all_to_all(
        words, "table", split_axis=0, concat_axis=0, tiled=True, axis_index_groups=sides
    )
    vectors = tuple(map(row, (imp_user, labels, b_hidden, b_cross, norm_gain, w_score)))
    with jax.named_scope("count"):
        counts = kernel_call(
            lambda *refs: count_kernel(users, *refs),
            jax.ShapeDtypeStruct((2 * (table_count // DEPTH), chips * users, DEPTH), BF16),
            1 << 33,
        )(words, *vectors)
    with jax.named_scope("pool"):
        partials = kernel_call(
            pool_kernel, jax.ShapeDtypeStruct((chips, users, width), BF16), 1 << 30
        )(counts, table_rows, other_rows)
    imp_row, label_row, b_hidden, b_cross, norm_gain, w_score = vectors
    returned = lax.all_to_all(
        partials, "table", split_axis=0, concat_axis=0, tiled=True, axis_index_groups=sides
    )
    pooled_user = (jnp.sum(returned.astype(F32), axis=0) * float(history) ** (-0.5)).astype(BF16)
    group_rows = lax.all_to_all(
        jnp.broadcast_to(pooled_user[None], (samples, users, width)),
        "sample",
        split_axis=0,
        concat_axis=0,
        tiled=True,
    ).reshape(samples * users, width)
    with jax.named_scope("dense"):
        scores, item_grad, per_user = kernel_call(
            dense_kernel,
            (
                jax.ShapeDtypeStruct((1, imps), F32),
                jax.ShapeDtypeStruct((imps, width), F32),
                jax.ShapeDtypeStruct((samples * users, width), BF16),
            ),
            1 << 30,
        )(
            group_rows,
            imp_row,
            item_rows,
            label_row,
            w_hidden,
            b_hidden,
            w_back,
            w_cross,
            b_cross,
            norm_gain,
            w_score,
        )
    parts = lax.all_to_all(
        per_user.reshape(samples, users, width), "sample", split_axis=0, concat_axis=0, tiled=True
    )
    with jax.named_scope("finish"):
        user_grad, item_grad, scores, pooled_user = kernel_call(
            finish_kernel,
            (jax.ShapeDtypeStruct((users, width), F32), like(item_grad), like(scores), like(pooled_user)),
            1 << 20,
            in_specs=[VMEM] * 4,
            out_specs=[HBM] * 4,
            scratch=[pltpu.VMEM((users, width), F32), pltpu.SemaphoreType.DMA((4,))],
        )(parts, item_grad, scores, pooled_user)
    return (pooled_user, scores.reshape(-1), user_grad, item_grad)


def solution(mesh):
    both = ("table", "sample")
    in_specs = (
        P(both, None, None),
        P(both, None),
        P("table", None),
        P(both),
        P(both, None),
        P(both),
    ) + (P(),) * 7
    out_specs = (P(both, None), P(both), P(both, None), P(both, None))
    return jax.shard_map(body, mesh=mesh, in_specs=in_specs, out_specs=out_specs, check_vma=False)
```

```python
import jax
import jax.numpy as jnp
from jax import lax
from jax.experimental import pallas as pl
from jax.experimental.pallas import tpu as pltpu
from jax.sharding import PartitionSpec as P

F32 = jnp.float32
BF16 = jnp.bfloat16
F8 = jnp.float8_e4m3fn
LOW_BITS = 7
LOW = 1 << LOW_BITS
DEPTH = 256
VMEM_LIMIT = 32 * 1024 * 1024


def rows_by_rows(a, b):
    return lax.dot_general(a, b, (((1,), (1,)), ((), ())), preferred_element_type=F32)


def pack_words(ids, lens):
    live = lax.broadcasted_iota(jnp.int32, ids.shape, 1) < lens[:, None, :]
    ids = jnp.where(live, ids, -1)
    half = ids.shape[0] // 2
    return (ids[:half] & 0xFFFF) | (ids[half:] << 16)


def turn_kernel(words_ref, out_ref):
    half, slots, shards = words_ref.shape
    words = words_ref[...].reshape(half * slots, shards).T
    chips, cores, _ = out_ref.shape
    for chip in range(chips):
        out_ref[chip] = words[chip * cores : (chip + 1) * cores]


def count_kernel(users, words_ref, *refs):
    counts_ref = refs[-1]
    sources, _, positions = words_ref.shape
    half = users // 2
    side_by_side = counts_ref.shape[2] // LOW
    highs = counts_ref.shape[0] // 2 * side_by_side
    core = lax.rem(lax.axis_index("table"), 2)
    user_of = lax.broadcasted_iota(jnp.int32, (1, positions), 1) // (positions // half)
    high_rows = lax.broadcasted_iota(jnp.int32, (highs * half, positions), 0).astype(jnp.int8)
    low_rows = lax.broadcasted_iota(jnp.int32, (LOW, positions), 0).astype(jnp.int8)
    one, zero = jnp.ones((), F8), jnp.zeros((), F8)

    def count(source, carry):
        pair = words_ref[source]
        target = pl.ds(pl.multiple_of(source * users, users), users)
        codes = []
        for ids in (pair & 0xFFFF, (pair >> 16) & 0xFFFF):
            low = jnp.where(ids < highs * LOW, ids & (LOW - 1), -1)
            codes.append((((ids >> LOW_BITS) & (highs - 1)) * half + user_of, low))
        for shard in range(2):
            halves = []
            for high, low in codes:
                high_hot = jnp.where(high[shard : shard + 1].astype(jnp.int8) == high_rows, one, zero)
                low_hot = jnp.where(low[shard : shard + 1].astype(jnp.int8) == low_rows, one, zero)
                halves.append(rows_by_rows(high_hot, low_hot))
            first_part = (core ^ shard) * (highs // side_by_side)
            for part in range(highs):
                rows = slice(part * half, (part + 1) * half)
                lane = part % side_by_side * LOW
                counts_ref[first_part + part // side_by_side, target, lane : lane + LOW] = jnp.concatenate(
                    [counts[rows] for counts in halves], axis=0
                ).astype(BF16)
        return carry

    lax.fori_loop(0, sources, count, 0, unroll=32)


def pool_kernel(counts_ref, own_ref, other_ref, out_ref):
    parts, _, depth = counts_ref.shape
    sources, users, width = out_ref.shape
    chunk = 16
    for first in range(0, sources, chunk):
        total = None
        for part in range(parts):
            shard_ref = (own_ref, other_ref)[part // (parts // 2)]
            low_row = part % (parts // 2) * depth
            term = jnp.dot(
                counts_ref[part, first * users : (first + chunk) * users, :],
                shard_ref[low_row : low_row + depth, :],
                preferred_element_type=F32,
            )
            total = term if total is None else total + term
        out_ref[first : first + chunk] = total.astype(BF16).reshape(chunk, users, width)


def dense_kernel(
    rows_ref,
    imp_ref,
    item_ref,
    labels_ref,
    w_hidden_ref,
    b_hidden_ref,
    w_back_ref,
    w_cross_ref,
    b_cross_ref,
    gain_ref,
    w_score_ref,
    scores_ref,
    item_grad_ref,
    per_user_ref,
):
    group_users, width = rows_ref.shape
    imps = item_ref.shape[0]
    picks_t = jnp.where(
        lax.broadcasted_iota(jnp.int32, (group_users, imps), 0) == imp_ref[...], 1.0, 0.0
    ).astype(F32)
    picks = picks_t.T.astype(BF16)
    picks_t = picks_t.astype(BF16)
    user_feat = jnp.dot(picks, rows_ref[...], preferred_element_type=F32).astype(BF16)
    joined = jnp.concatenate([user_feat, item_ref[...]], axis=1)
    lifted = joined.astype(F32)
    pre = jnp.dot(joined, w_hidden_ref[...], preferred_element_type=F32) + b_hidden_ref[...]
    factor = jnp.dot(joined, w_cross_ref[...], preferred_element_type=F32) + (b_cross_ref[...] + 1.0)
    k, c = 0.7978845608028654, 0.044715
    square = pre * pre
    half_tanh = 0.5 * jnp.tanh(pre * (k + (k * c) * square))
    cdf = 0.5 + half_tanh
    hidden = (pre * cdf).astype(BF16)
    slope = cdf + (cdf * (0.5 - half_tanh)) * (pre * (2.0 * k + (6.0 * k * c) * square))
    summed = jnp.dot(hidden, w_back_ref[...], preferred_element_type=F32) + lifted * factor
    columns = summed.shape[1]
    centred = summed - jnp.sum(summed, axis=1, keepdims=True) * (1.0 / columns)
    variance = jnp.sum(centred * centred, axis=1, keepdims=True) * (1.0 / columns)
    scale = lax.rsqrt(variance + 1e-05)
    weight = gain_ref[...] * w_score_ref[...]
    scores = scale * jnp.sum(centred * weight, axis=1, keepdims=True)
    scores_ref[...] = jnp.broadcast_to(scores, (imps, 128)).T[:1]
    labels = jnp.broadcast_to(labels_ref[...].astype(F32), (8, imps)).T[:, :1]
    score_grad = 1.0 / (1.0 + jnp.exp(-scores)) - labels
    flat = weight - jnp.sum(weight, axis=1, keepdims=True) * (1.0 / columns)
    summed_grad = (score_grad * scale) * (flat - centred * (scale * scores * (1.0 / columns)))
    hidden_grad = rows_by_rows(summed_grad.astype(BF16), w_back_ref[...])
    pre_grad = (hidden_grad * slope).astype(BF16)
    cross_grad = (summed_grad * lifted).astype(BF16)
    joined_grad = (
        summed_grad * factor
        + rows_by_rows(pre_grad, w_hidden_ref[...])
        + rows_by_rows(cross_grad, w_cross_ref[...])
    )
    item_grad_ref[...] = joined_grad[:, width:]
    user_part = joined_grad[:, :width].astype(BF16)
    per_user_ref[...] = jnp.dot(picks_t, user_part, preferred_element_type=F32).astype(BF16)


def finish_kernel(parts_ref, item_ref, scores_ref, pooled_ref, user_hbm, item_hbm, scores_hbm, pooled_hbm, sums_ref, sems):
    copies = [
        pltpu.make_async_copy(item_ref, item_hbm, sems.at[0]),
        pltpu.make_async_copy(scores_ref, scores_hbm, sems.at[1]),
        pltpu.make_async_copy(pooled_ref, pooled_hbm, sems.at[2]),
    ]
    for copy in copies:
        copy.start()
    sums_ref[...] = jnp.sum(parts_ref[...].astype(F32), axis=0)
    copies.append(pltpu.make_async_copy(sums_ref, user_hbm, sems.at[3]))
    copies[-1].start()
    for copy in copies:
        copy.wait()


HBM = pl.BlockSpec(memory_space=pltpu.HBM)
VMEM = pl.BlockSpec(memory_space=pltpu.VMEM)


def kernel_call(kernel, out_shape, flops, in_specs=None, out_specs=None, scratch=()):
    specs = {}
    if in_specs is not None:
        specs["in_specs"] = in_specs
    if out_specs is not None:
        specs["out_specs"] = out_specs
    return pl.pallas_call(
        kernel,
        out_shape=out_shape,
        scratch_shapes=list(scratch),
        compiler_params=pltpu.CompilerParams(vmem_limit_bytes=VMEM_LIMIT),
        cost_estimate=pl.CostEstimate(flops=flops, bytes_accessed=1 << 21, transcendentals=0),
        **specs,
    )


def body(
    hist_ids,
    hist_lens,
    table_rows,
    imp_user,
    item_rows,
    labels,
    w_hidden,
    b_hidden,
    w_back,
    w_cross,
    b_cross,
    norm_gain,
    w_score,
):
    users, sources, slots = hist_ids.shape
    table_count, width = table_rows.shape
    samples = lax.axis_size("sample")
    imps = imp_user.shape[0]
    history = slots * sources * 2 // 3
    like = lambda array: jax.ShapeDtypeStruct(array.shape, array.dtype)
    row = lambda vector: vector.reshape(1, -1)
    chips = sources // 2
    sides = [[2 * chip + core for chip in range(chips)] for core in range(2)]
    with jax.named_scope("pack_ids"):
        words = pack_words(jnp.transpose(hist_ids, (0, 2, 1)), hist_lens)
        words = kernel_call(
            turn_kernel,
            jax.ShapeDtypeStruct((chips, 2, users * slots // 2), jnp.int32),
            1 << 34,
        )(words)
    other_rows = lax.ppermute(table_rows, "table", [(i, i ^ 1) for i in range(sources)])
    words = lax.all_to_all(
        words, "table", split_axis=0, concat_axis=0, tiled=True, axis_index_groups=sides
    )
    vectors = tuple(map(row, (imp_user, labels, b_hidden, b_cross, norm_gain, w_score)))
    with jax.named_scope("count"):
        counts = kernel_call(
            lambda *refs: count_kernel(users, *refs),
            jax.ShapeDtypeStruct((2 * (table_count // DEPTH), chips * users, DEPTH), BF16),
            1 << 33,
        )(words, *vectors)
    with jax.named_scope("pool"):
        partials = kernel_call(
            pool_kernel, jax.ShapeDtypeStruct((chips, users, width), BF16), 1 << 30
        )(counts, table_rows, other_rows)
    imp_row, label_row, b_hidden, b_cross, norm_gain, w_score = vectors
    returned = lax.all_to_all(
        partials, "table", split_axis=0, concat_axis=0, tiled=True, axis_index_groups=sides
    )
    pooled_user = (jnp.sum(returned.astype(F32), axis=0) * float(history) ** (-0.5)).astype(BF16)
    group_rows = lax.all_to_all(
        jnp.broadcast_to(pooled_user[None], (samples, users, width)),
        "sample",
        split_axis=0,
        concat_axis=0,
        tiled=True,
    ).reshape(samples * users, width)
    with jax.named_scope("dense"):
        scores, item_grad, per_user = kernel_call(
            dense_kernel,
            (
                jax.ShapeDtypeStruct((1, imps), F32),
                jax.ShapeDtypeStruct((imps, width), F32),
                jax.ShapeDtypeStruct((samples * users, width), BF16),
            ),
            1 << 30,
        )(
            group_rows,
            imp_row,
            item_rows,
            label_row,
            w_hidden,
            b_hidden,
            w_back,
            w_cross,
            b_cross,
            norm_gain,
            w_score,
        )
    parts = lax.all_to_all(
        per_user.reshape(samples, users, width), "sample", split_axis=0, concat_axis=0, tiled=True
    )
    with jax.named_scope("finish"):
        user_grad, item_grad, scores, pooled_user = kernel_call(
            finish_kernel,
            (jax.ShapeDtypeStruct((users, width), F32), like(item_grad), like(scores), like(pooled_user)),
            1 << 20,
            in_specs=[VMEM] * 4,
            out_specs=[HBM] * 4,
            scratch=[pltpu.VMEM((users, width), F32), pltpu.SemaphoreType.DMA((4,))],
        )(parts, item_grad, scores, pooled_user)
    return (pooled_user, scores.reshape(-1), user_grad, item_grad)


def solution(mesh):
    both = ("table", "sample")
    in_specs = (
        P(both, None, None),
        P(both, None),
        P("table", None),
        P(both),
        P(both, None),
        P(both),
    ) + (P(),) * 7
    out_specs = (P(both, None), P(both), P(both, None), P(both, None))
    return jax.shard_map(body, mesh=mesh, in_specs=in_specs, out_specs=out_specs, check_vma=False)
```
